256 devices in a mesh: blk: 16 (over x_hi, y, core), loop: 16 (over x_lo, z).
Axes of the slice: x: 4 (x_hi: 2, x_lo: 2; x = x_hi * 2 + x_lo), y: 4, z: 8, core: 2. Of those that a mesh axis runs over, the one named last changes fastest.
Arguments:
- points: bfloat16 [3072, 1024], P('blk'), may hold values from -6 to 6
- centroids: bfloat16 [262144, 1024], P(('blk', 'loop')), may hold values from -0.03125 to 0.03125
Outputs:
- new_centroids: bfloat16 [262144, 1024], P(('blk', 'loop'))
- normalizer: float32 [3072], P('blk')
The draws below stay inside these ranges and needn't reach their ends.
All inputs are finite; a program needn't handle non-finite values.
Results may differ from the reference program's by a relative error of at most 0.0049.
Values may be sent and summed in bfloat16 or wider, within the bound.
A program may use at most 64 MiB of HBM per device.

```python
import jax
import jax.numpy as jnp
from jax import lax

D = 1024
CB = 1024
EMBEDDING_COUNT = 3072
K = 262144
N_BLK = 16


def centroid_row(key, index):
    signs = jax.random.bernoulli(jax.random.fold_in(key, index), 0.5, (D,))
    return jnp.where(signs, 1.0, -1.0).astype(jnp.float32) / 32.0


def draw_centroids(key, part):
    rows = jax.vmap(lambda index: centroid_row(key, index))(jnp.arange(K))
    return rows.astype(jnp.bfloat16)


def drawn_rows(base, key):
    mixture_key, first_key, second_key, strength_key = jax.random.split(key, 4)
    chosen = jax.random.randint(mixture_key, (EMBEDDING_COUNT,), 0, 32) == 0
    chosen = chosen | (jnp.arange(EMBEDDING_COUNT) % 32 == 0)
    first = jax.random.randint(first_key, (EMBEDDING_COUNT,), 0, K)
    second = (first + 1 + jax.random.randint(second_key, (EMBEDDING_COUNT,), 0, K - 1)) % K
    strength = 6.0 * jax.random.randint(strength_key, (EMBEDDING_COUNT, 1), 1, 4).astype(jnp.float32)
    rows_one = jax.vmap(lambda index: centroid_row(base, index))(first)
    rows_two = jax.vmap(lambda index: centroid_row(base, index))(second)
    aligned = strength * rows_one + (strength - 0.1) * rows_two
    return (chosen, aligned)


def draw_points(key, part):
    base = key
    key = jax.random.fold_in(key, 7)
    drawn_key = jax.random.fold_in(key, 0)
    align_key = jax.random.fold_in(key, 2)
    chosen, aligned = drawn_rows(base, align_key)
    drawn = jnp.clip(jax.random.normal(drawn_key, (EMBEDDING_COUNT, D), jnp.float32), -6.0, 6.0)
    values = jnp.where(chosen[:, None], aligned, drawn)
    return values.astype(jnp.bfloat16)


def setup_inputs(seed: int = 0) -> dict:
    key_of = jax.random.split(jax.random.key(seed), 3)
    points = draw_points(jax.random.fold_in(key_of[2], 71), 0)
    centroids = draw_centroids(jax.random.fold_in(key_of[2], 71), 0)
    return dict(points=points, centroids=centroids)


def block_scores(points, block):
    return lax.dot_general(points, block, (((1,), (1,)), ((), ())), preferred_element_type=jnp.float32) * 20.0


def reference(points, centroids):
    width = CB * N_BLK
    blocks = centroids.reshape(K // width, width, D)

    def partial_lse(block):
        return jax.nn.logsumexp(block_scores(points, block), axis=1)

    normalizer = jax.nn.logsumexp(lax.map(partial_lse, blocks), axis=0)
    eta = float(K) / float(EMBEDDING_COUNT)

    def update(block):
        weights = jnp.exp(block_scores(points, block) - normalizer[:, None])
        loads = jnp.sum(weights, axis=0)
        rounded = weights.astype(jnp.bfloat16)
        sums = lax.dot_general(rounded, points, (((0,), (0,)), ((), ())), preferred_element_type=jnp.float32)
        fresh = (block.astype(jnp.float32) + eta * sums) / (1.0 + eta * loads)[:, None]
        return fresh.astype(jnp.bfloat16)

    new_centroids = lax.map(update, blocks).reshape(K, D)
    return new_centroids, normalizer
```

```python
import functools

import jax
import jax.numpy as jnp
from jax import lax
from jax.experimental import pallas as pl
from jax.experimental.pallas import tpu as pltpu
from jax.sharding import PartitionSpec as P

MESH = pl.DeviceIdType.MESH
NT = (((1,), (1,)), ((), ()))
LOG2E = 1.4426950408889634
LN2 = 0.6931471805599453
SCALE = 20.0 * LOG2E
NB = 16
CHUNKS = 6
AHEAD = 6


def merge(parts):
    top = jnp.max(parts, axis=0)
    return top + jnp.log2(jnp.sum(jnp.exp2(parts - top[None]), axis=0))


def kernel(
    eta, p_hbm, c_hbm, o_ref, n_ref,
    g, cent, s, acc, ld, ra, rb,
    load_sem, cent_sem, d1_send, d1_recv, sh_send, sh_recv, sib_send, sib_recv,
    a_send, a_recv, b_send, b_recv,
):
    count, width = p_hbm.shape
    rows = count // CHUNKS
    chunk = NB * rows
    lanes = 128
    groups = chunk // lanes
    half, quarter = width // 2, width // 4
    b = lax.axis_index("blk")
    l = lax.axis_index("loop")
    xh, y, c = b // 8, (b // 2) % 4, b % 2
    xl, z = l // 8, l % 8
    up, down, far = (y + 1) % 4, (y + 3) % 4, (y + 2) % 4
    ox, ol = 1 - xh, 1 - xl

    def blk_of(hi, yy):
        return (hi * 4 + yy) * 2 + c

    def shard_rows(hi, yy):
        return pl.ds(pl.multiple_of(c * (8 * rows) + (hi * 4 + yy) * rows, rows), rows)

    def cols_half(kind):
        return pl.ds(pl.multiple_of(kind * half, half), half)

    def cols_quarter(kind):
        return pl.ds(pl.multiple_of(kind * quarter, quarter), quarter)

    own = shard_rows(xh, y)
    for k in range(CHUNKS):
        pltpu.make_async_copy(p_hbm.at[pl.ds(k * rows, rows)], g.at[k, own], load_sem).start()
    cent_copy = pltpu.make_async_copy(c_hbm, cent, cent_sem)
    cent_copy.start()

    barrier = pltpu.get_barrier_semaphore()
    peers = [((b + j) % NB, l) for j in range(1, NB)]
    peers += [(b, (l + j) % NB) for j in range(1, NB)]
    peers += [(blk_of(ox, (y + j) % 4), ol * 8 + z) for j in range(4)]
    for peer in peers:
        pl.semaphore_signal(barrier, inc=1, device_id=peer, device_id_type=MESH)
    pl.semaphore_wait(barrier, len(peers))

    def wait_bytes(like, sem):
        pltpu.make_async_copy(like, like, sem).wait()

    my_half, my_quarter = (z + xl) % 2, (z + 2 * xl) % 4
    x_half, x_quarter = (z + ol) % 2, (z + 2 * ol) % 4
    x_loop = ol * 8 + z
    direct = [
        (blk_of(ox, down), x_loop, cols_quarter(x_quarter)),
        (blk_of(ox, up), x_loop, cols_quarter(x_quarter)),
        (blk_of(ox, far), x_loop, cols_quarter(x_quarter)),
        (blk_of(xh, far), l, cols_quarter(my_quarter)),
        (blk_of(xh, down), l, cols_half(my_half)),
        (blk_of(xh, up), l, cols_half(my_half)),
        (blk_of(ox, y), x_loop, cols_half(x_half)),
    ]
    z_up, z_down, x_same = xl * 8 + (z + 1) % 8, xl * 8 + (z + 7) % 8, ol * 8 + z
    arriving = [
        (shard_rows(ox, up), cols_quarter(my_quarter), (z_up, z_down, x_same)),
        (shard_rows(ox, down), cols_quarter(my_quarter), (z_up, z_down, x_same)),
        (shard_rows(ox, far), cols_quarter(my_quarter), (z_up, z_down, x_same)),
        (shard_rows(xh, far), cols_quarter(my_quarter), (z_up, z_down, x_same)),
        (shard_rows(xh, up), cols_half(my_half), (z_up,)),
        (shard_rows(xh, down), cols_half(my_half), (z_down,)),
        (shard_rows(ox, y), cols_half(my_half), (x_same,)),
    ]
    direct_bytes_rows = rows * 5 // 2
    share_bytes_rows = rows * 9 // 2

    def start_direct(k):
        for i, (tb, tl, cols) in enumerate(direct):
            pltpu.make_async_remote_copy(
                src_ref=g.at[k, own, cols], dst_ref=g.at[k, own, cols],
                send_sem=d1_send.at[k], recv_sem=d1_recv.at[k, i],
                device_id=(tb, tl), device_id_type=MESH,
            ).start()

    def share(k):
        for i, (rws, cols, targets) in enumerate(arriving):
            piece = g.at[k, rws, cols]
            wait_bytes(piece, d1_recv.at[k, i])
            for target in targets:
                pltpu.make_async_remote_copy(
                    src_ref=piece, dst_ref=piece,
                    send_sem=sh_send.at[k], recv_sem=sh_recv.at[k],
                    device_id=(b, target), device_id_type=MESH,
                ).start()

    mine = pl.ds(pl.multiple_of(c * (8 * rows), 8 * rows), 8 * rows)
    theirs = pl.ds(pl.multiple_of((1 - c) * (8 * rows), 8 * rows), 8 * rows)
    sibling = (b + 1 - 2 * c, l)

    def to_sibling(k):
        wait_bytes(p_hbm.at[pl.ds(0, share_bytes_rows)], sh_recv.at[k])
        pltpu.make_async_remote_copy(
            src_ref=g.at[k, mine], dst_ref=g.at[k, mine],
            send_sem=sib_send.at[k], recv_sem=sib_recv.at[k],
            device_id=sibling, device_id_type=MESH,
        ).start()

    tile = 256

    def scores(k):
        wait_bytes(g.at[k, theirs], sib_recv.at[k])
        top, total = None, None
        for m0 in range(0, width, tile):
            t = lax.dot_general(cent[m0:m0 + tile, :], g[k], NT, preferred_element_type=jnp.float32)
            s[k, m0:m0 + tile, :] = t
            t = t * SCALE
            high = jnp.max(jnp.max(t.reshape(tile // 8, 8, chunk), axis=0), axis=0, keepdims=True)
            new = high if top is None else jnp.maximum(top, high)
            part = jnp.sum(jnp.exp2(t - new).reshape(tile // 8, 8, chunk), axis=0)
            total = part if total is None else total * jnp.exp2(top - new) + part
            top = new
        lse = top + jnp.log2(jnp.sum(total, axis=0, keepdims=True))
        for q in range(groups):
            ra[k, l, q:q + 1, :] = lse[:, q * lanes:(q + 1) * lanes]
        for j in range(1, NB):
            pltpu.make_async_remote_copy(
                src_ref=ra.at[k, l], dst_ref=ra.at[k, l],
                send_sem=a_send.at[k], recv_sem=a_recv.at[k],
                device_id=(b, (l + j) % NB), device_id_type=MESH,
            ).start()

    def first_merge(k):
        wait_bytes(ra.at[k, pl.ds(0, NB - 1)], a_recv.at[k])
        rb[k, b] = merge(ra[k])
        for j in range(1, NB):
            pltpu.make_async_remote_copy(
                src_ref=rb.at[k, b], dst_ref=rb.at[k, b],
                send_sem=b_send.at[k], recv_sem=b_recv.at[k],
                device_id=((b + j) % NB, l), device_id_type=MESH,
            ).start()

    def sums(k):
        wait_bytes(rb.at[k, pl.ds(0, NB - 1)], b_recv.at[k])
        norm = merge(rb[k])
        n_ref[k] = norm * LN2
        line = jnp.concatenate([norm[q:q + 1, :] for q in range(groups)], axis=1)
        for m0 in range(0, width, tile):
            at = pl.ds(m0, tile)
            w = jnp.exp2(s[k, at, :] * SCALE - line)
            load = w[:, 0:lanes]
            for q in range(1, groups):
                load = load + w[:, q * lanes:(q + 1) * lanes]
            part = jnp.dot(w.astype(jnp.bfloat16), g[k], preferred_element_type=jnp.float32)
            if k > 0:
                load = load + ld[at, :]
                part = part + acc[at, :]
            if k < CHUNKS - 1:
                ld[at, :] = load
                acc[at, :] = part
            else:
                scale = 1.0 / (1.0 + eta * jnp.sum(load, axis=1, keepdims=True))
                fresh = (cent[at, :].astype(jnp.float32) + eta * part) * scale
                o_ref[at, :] = fresh.astype(jnp.bfloat16)

    wait_bytes(p_hbm, load_sem)
    for k in range(min(AHEAD, CHUNKS)):
        start_direct(k)
    for t in range(CHUNKS + 2):
        if t < CHUNKS:
            if t + AHEAD < CHUNKS:
                start_direct(t + AHEAD)
            share(t)
        if 0 <= t - 1 < CHUNKS:
            to_sibling(t - 1)
        if t == 2:
            cent_copy.wait()
        if 0 <= t - 2 < CHUNKS:
            scores(t - 2)
        if 0 <= t - 4 < CHUNKS:
            first_merge(t - 4)
    sums(0)
    first_merge(CHUNKS - 2)
    sums(1)
    first_merge(CHUNKS - 1)
    for k in range(2, CHUNKS):
        sums(k)

    for k in range(CHUNKS):
        wait_bytes(p_hbm.at[pl.ds(0, direct_bytes_rows)], d1_send.at[k])
        wait_bytes(p_hbm.at[pl.ds(0, share_bytes_rows)], sh_send.at[k])
        wait_bytes(g.at[k, mine], sib_send.at[k])
        wait_bytes(ra.at[k, pl.ds(0, NB - 1)], a_send.at[k])
        wait_bytes(rb.at[k, pl.ds(0, NB - 1)], b_send.at[k])


def per_device(points, centroids):
    count, width = points.shape
    held = centroids.shape[0]
    total = count * NB
    eta = float(held * NB * NB) / float(total)
    rows = count // CHUNKS
    chunk = NB * rows
    groups = chunk // 128
    dma = pltpu.SemaphoreType.DMA
    fresh, norm = pl.pallas_call(
        functools.partial(kernel, eta),
        out_shape=(
            jax.ShapeDtypeStruct((held, width), jnp.bfloat16),
            jax.ShapeDtypeStruct((CHUNKS, groups, 128), jnp.float32),
        ),
        in_specs=[pl.BlockSpec(memory_space=pl.ANY)] * 2,
        out_specs=(pl.BlockSpec(memory_space=pltpu.VMEM), pl.BlockSpec(memory_space=pltpu.VMEM)),
        scratch_shapes=[
            pltpu.VMEM((CHUNKS, chunk, width), jnp.bfloat16),
            pltpu.VMEM((held, width), jnp.bfloat16),
            pltpu.VMEM((CHUNKS, held, chunk), jnp.float32),
            pltpu.VMEM((held, width), jnp.float32),
            pltpu.VMEM((held, 128), jnp.float32),
            pltpu.VMEM((CHUNKS, NB, groups, 128), jnp.float32),
            pltpu.VMEM((CHUNKS, NB, groups, 128), jnp.float32),
            dma, dma,
            dma((CHUNKS,)), dma((CHUNKS, 7)),
            dma((CHUNKS,)), dma((CHUNKS,)),
            dma((CHUNKS,)), dma((CHUNKS,)),
            dma((CHUNKS,)), dma((CHUNKS,)),
            dma((CHUNKS,)), dma((CHUNKS,)),
        ],
        compiler_params=pltpu.CompilerParams(
            collective_id=0, has_side_effects=True, vmem_limit_bytes=48 * 1024 * 1024
        ),
        cost_estimate=pl.CostEstimate(
            flops=4 * total * held * width, bytes_accessed=6 * held * width, transcendentals=2 * total * held
        ),
    )(points, centroids)
    b = lax.axis_index("blk")
    start = (b % 2) * (8 * rows) + (b // 2) * rows
    own = lax.dynamic_slice_in_dim(norm.reshape(CHUNKS, chunk), start, rows, 1)
    return fresh, own.reshape(count)


def solution(mesh):
    placed = (P("blk", None), P(("blk", "loop"), None))
    return jax.shard_map(
        per_device,
        mesh=mesh,
        in_specs=placed,
        out_specs=(P(("blk", "loop"), None), P("blk")),
        check_vma=False,
    )
```

```python
import functools

import jax
import jax.numpy as jnp
from jax import lax
from jax.experimental import pallas as pl
from jax.experimental.pallas import tpu as pltpu
from jax.sharding import PartitionSpec as P

MESH = pl.DeviceIdType.MESH
NT = (((1,), (1,)), ((), ()))
LOG2E = 1.4426950408889634
LN2 = 0.6931471805599453
SCALE = 20.0 * LOG2E
NB = 16
SIZES = (64, 64, 64)
STARTS = (("Q", 0), ("Q", 1), ("Q", 2), ("F", 0), ("F", 1), ("F", 2))
STEPS = (
    ("share", 0), ("share", 1), ("share", 2),
    ("pass", 0), ("own", 0), ("sib", 0), ("tell", 0),
    ("pass", 1), ("own", 1), ("merge", 0), ("sib", 1), ("tell", 1),
    ("pass", 2), ("own", 2), ("sib", 2), ("tell", 2),
    ("merge", 1), ("sums", 0), ("merge", 2), ("sums", 1), ("sums", 2),
)

def merge(parts):
    top = jnp.max(parts, axis=0)
    return top + jnp.log2(jnp.sum(jnp.exp2(parts - top[None]), axis=0))


def kernel(eta, p_hbm, c_hbm, o_ref, n_ref, g, cent, acc, ld, *rest):
    chunks = len(SIZES)
    s, ra, rb = rest[:chunks], rest[chunks:2 * chunks], rest[2 * chunks:3 * chunks]
    (
        load_sem, cent_sem, q_recv, f_recv, d_send, sh_send, sh_recv, sib_send, sib_recv,
        a_send, a_recv, b_send, b_recv,
    ) = rest[3 * chunks:]
    count, width = p_hbm.shape
    held = cent.shape[0]
    lanes = 128
    quarter = width // 4
    b = lax.axis_index("blk")
    l = lax.axis_index("loop")
    xh, y, c = b // 8, (b // 2) % 4, b % 2
    xl, z = l // 8, l % 8
    up, down, far = (y + 1) % 4, (y + 3) % 4, (y + 2) % 4
    ox, ol = 1 - xh, 1 - xl
    sc = 1 - c
    shard = xh * 4 + y

    def blk_of(hi, yy):
        return (hi * 4 + yy) * 2 + c

    def first_row(k):
        return NB * sum(SIZES[:k])

    def shard_rows(k, hi, yy):
        rows = SIZES[k]
        return pl.ds(pl.multiple_of(first_row(k) + c * (8 * rows) + (hi * 4 + yy) * rows, 16), rows)

    def core_rows(k, core):
        rows = SIZES[k]
        return pl.ds(pl.multiple_of(first_row(k) + core * (8 * rows), 16), 8 * rows)

    def cols_quarter(kind):
        return pl.ds(pl.multiple_of(kind * quarter, quarter), quarter)

    for k, rows in enumerate(SIZES):
        pltpu.make_async_copy(
            p_hbm.at[pl.ds(sum(SIZES[:k]), rows)], g.at[shard_rows(k, xh, y)], load_sem
        ).start()
    cent_copy = pltpu.make_async_copy(c_hbm, cent, cent_sem)
    cent_copy.start()

    loop_order = [4, 12, 3, 5, 11, 13, 2, 6, 10, 14, 1, 7, 9, 15, 8]
    blk_order = [12, 4, 11, 13, 3, 5, 8, 9, 10, 14, 2, 6, 7, 15, 1]
    loop_peers = [(b, (l + j) % NB) for j in loop_order]
    blk_peers = [((b + j) % NB, l) for j in blk_order]
    x_loop = ol * 8 + z
    x_peers = [(blk_of(ox, (y + j) % 4), x_loop) for j in (2, 1, 3, 0)]
    barrier = pltpu.get_barrier_semaphore()
    for peer in loop_peers + blk_peers + x_peers:
        pl.semaphore_signal(barrier, inc=1, device_id=peer, device_id_type=MESH)
    pl.semaphore_wait(barrier, 2 * (NB - 1) + 4)

    def wait_bytes(like, sem):
        pltpu.make_async_copy(like, like, sem).wait()

    def send(piece, send_sem, recv_sem, peer):
        pltpu.make_async_remote_copy(
            src_ref=piece, dst_ref=piece, send_sem=send_sem, recv_sem=recv_sem,
            device_id=peer, device_id_type=MESH,
        ).start()

    my_quarter = cols_quarter((z + 2 * xl) % 4)
    x_quarter = cols_quarter((z + 2 * ol) % 4)
    parted = [
        ((blk_of(ox, down), x_loop), x_quarter, (ox, up)),
        ((blk_of(ox, up), x_loop), x_quarter, (ox, down)),
        ((blk_of(ox, far), x_loop), x_quarter, (ox, far)),
        ((blk_of(xh, far), l), my_quarter, (xh, far)),
    ]
    near = [(blk_of(xh, down), l), (blk_of(xh, up), l), (blk_of(ox, y), x_loop)]
    sharers = [(b, xl * 8 + (z + 1) % 8), (b, xl * 8 + (z + 7) % 8), (b, x_loop)]
    sibling = (b + 1 - 2 * c, l)

    def start_parted(k):
        for i, (peer, cols, _) in enumerate(parted):
            send(g.at[shard_rows(k, xh, y), cols], d_send.at[k], q_recv.at[k, i], peer)

    def start_near(k):
        for peer in near:
            send(g.at[shard_rows(k, xh, y)], d_send.at[k], f_recv.at[k], peer)

    def share(k):
        for i, (_, _, source) in enumerate(parted):
            piece = g.at[shard_rows(k, *source), my_quarter]
            wait_bytes(piece, q_recv.at[k, i])
            for peer in sharers:
                send(piece, sh_send.at[k], sh_recv.at[k], peer)

    def to_sibling(k):
        wait_bytes(g.at[pl.ds(0, 3 * SIZES[k])], f_recv.at[k])
        wait_bytes(g.at[pl.ds(0, 3 * SIZES[k])], sh_recv.at[k])
        send(g.at[core_rows(k, c)], sib_send.at[k], sib_recv.at[k], sibling)

    tile = 256

    def scores(k, core):
        part = 8 * SIZES[k]
        top, total = None, None
        for m0 in range(0, held, tile):
            t = lax.dot_general(
                cent[m0:m0 + tile, :], g[core_rows(k, core), :], NT, preferred_element_type=jnp.float32
            )
            s[k][core, m0:m0 + tile, :] = t
            t = t * SCALE
            high = jnp.max(jnp.max(t.reshape(tile // 8, 8, part), axis=0), axis=0, keepdims=True)
            new = high if top is None else jnp.maximum(top, high)
            add = jnp.sum(jnp.exp2(t - new).reshape(tile // 8, 8, part), axis=0)
            total = add if total is None else total * jnp.exp2(top - new) + add
            top = new
        lse = top + jnp.log2(jnp.sum(total, axis=0, keepdims=True))
        for q in range(part // lanes):
            ra[k][l, core, q:q + 1, :] = lse[:, q * lanes:(q + 1) * lanes]

    def sibling_scores(k):
        wait_bytes(g.at[core_rows(k, sc)], sib_recv.at[k])
        scores(k, sc)

    def tell(k):
        for peer in loop_peers:
            send(ra[k].at[l], a_send.at[k], a_recv.at[k], peer)

    def first_merge(k):
        wait_bytes(ra[k].at[pl.ds(0, NB - 1)], a_recv.at[k])
        rb[k][b] = merge(ra[k][...])
        for peer in blk_peers:
            send(rb[k].at[b], b_send.at[k], b_recv.at[k], peer)

    def sums(k):
        rows = SIZES[k]
        part = 8 * rows
        groups = part // lanes
        wait_bytes(rb[k].at[pl.ds(0, NB - 1)], b_recv.at[k])
        norm = merge(rb[k][...])
        lines = [
            jnp.concatenate([norm[h, q:q + 1, :] for q in range(groups)], axis=1) for h in range(2)
        ]
        for m0 in range(0, held, tile):
            at = pl.ds(m0, tile)
            w = jnp.concatenate([jnp.exp2(s[k][h, at, :] * SCALE - lines[h]) for h in range(2)], axis=1)
            load = w[:, 0:lanes]
            for q in range(1, 2 * groups):
                load = load + w[:, q * lanes:(q + 1) * lanes]
            add = jnp.dot(
                w.astype(jnp.bfloat16), g[pl.ds(first_row(k), NB * rows), :],
                preferred_element_type=jnp.float32,
            )
            if k > 0:
                load = load + ld[at, :]
                add = add + acc[at, :]
            if k < chunks - 1:
                ld[at, :] = load
                acc[at, :] = add
            else:
                scale = 1.0 / (1.0 + eta * jnp.sum(load, axis=1, keepdims=True))
                fresh = (cent[at, :].astype(jnp.float32) + eta * add) * scale
                o_ref[at, :] = fresh.astype(jnp.bfloat16)
        line = jnp.where(c == 0, lines[0], lines[1])
        for bit in range(3):
            turned = pltpu.roll(line, part - (rows << bit), 1)
            line = jnp.where((shard // (1 << bit)) % 2 == 1, turned, line)
        start = sum(SIZES[:k])
        n_ref[:, start:start + rows] = line[:, 0:rows] * LN2

    wait_bytes(p_hbm, load_sem)
    for kind, k in STARTS:
        start_parted(k) if kind == "Q" else start_near(k)
    cent_copy.wait()
    actions = dict(
        share=share, own=lambda k: scores(k, c), sib=sibling_scores, tell=tell,
        merge=first_merge, sums=sums,
    )
    actions["pass"] = to_sibling
    for kind, k in STEPS:
        actions[kind](k)

    for k, rows in enumerate(SIZES):
        wait_bytes(g.at[pl.ds(0, 4 * rows)], d_send.at[k])
        wait_bytes(g.at[pl.ds(0, 3 * rows)], sh_send.at[k])
        wait_bytes(g.at[core_rows(k, c)], sib_send.at[k])
        wait_bytes(ra[k].at[pl.ds(0, NB - 1)], a_send.at[k])
        wait_bytes(rb[k].at[pl.ds(0, NB - 1)], b_send.at[k])


def per_device(points, centroids):
    count, width = points.shape
    held = centroids.shape[0]
    total = count * NB
    eta = float(held * NB * NB) / float(total)
    chunks = len(SIZES)
    dma = pltpu.SemaphoreType.DMA
    hbm = pl.BlockSpec(memory_space=pltpu.HBM)
    vmem = pl.BlockSpec(memory_space=pltpu.VMEM)
    stats = [pltpu.VMEM((NB, 2, 8 * rows // 128, 128), jnp.float32) for rows in SIZES]
    each = dma((chunks,))
    fresh, norm = pl.pallas_call(
        functools.partial(kernel, eta),
        out_shape=(
            jax.ShapeDtypeStruct((held, width), jnp.bfloat16),
            jax.ShapeDtypeStruct((1, count), jnp.float32),
        ),
        in_specs=[hbm, hbm],
        out_specs=(vmem, vmem),
        scratch_shapes=[
            pltpu.VMEM((total, width), jnp.bfloat16),
            pltpu.VMEM((held, width), jnp.bfloat16),
            pltpu.VMEM((held, width), jnp.float32),
            pltpu.VMEM((held, 128), jnp.float32),
            *[pltpu.VMEM((2, held, 8 * rows), jnp.float32) for rows in SIZES],
            *stats, *stats,
            dma, dma,
            dma((chunks, 4)), each, each,
            each, each, each, each,
            each, each, each, each,
        ],
        compiler_params=pltpu.CompilerParams(
            collective_id=0, has_side_effects=True, vmem_limit_bytes=51 * 1024 * 1024
        ),
        cost_estimate=pl.CostEstimate(
            flops=4 * total * held * width, bytes_accessed=6 * held * width, transcendentals=2 * total * held
        ),
    )(points, centroids)
    return fresh, norm.reshape(count)


def solution(mesh):
    placed = (P("blk", None), P(("blk", "loop"), None))
    return jax.shard_map(
        per_device,
        mesh=mesh,
        in_specs=placed,
        out_specs=(P(("blk", "loop"), None), P("blk")),
        check_vma=False,
    )
```

```python
import functools

import jax
import jax.numpy as jnp
from jax import lax
from jax.experimental import pallas as pl
from jax.experimental.pallas import tpu as pltpu
from jax.sharding import PartitionSpec as P

MESH = pl.DeviceIdType.MESH
NT = (((1,), (1,)), ((), ()))
LOG2E = 1.4426950408889634
LN2 = 0.6931471805599453
SCALE = 20.0 * LOG2E
NB = 16
SIZES = (64, 64, 64)
STARTS = (("Q", 0), ("Q", 1), ("Q", 2), ("F", 0), ("F", 1), ("F", 2))
STEPS = (
    ("share", 0),
    ("share", 1),
    ("share", 2),
    ("pass", 0),
    ("own", 0),
    ("pass", 1),
    ("sib", 0),
    ("tell", 0),
    ("own", 1),
    ("pass", 2),
    ("sib", 1),
    ("tell", 1),
    ("own", 2),
    ("sib", 2),
    ("tell", 2),
    ("merge", 0),
    ("merge", 1),
    ("merge", 2),
    ("sums", 0),
    ("sums", 1),
    ("sums", 2),
)

def merge(parts):
    top = jnp.max(parts, axis=0)
    return top + jnp.log2(jnp.sum(jnp.exp2(parts - top[None]), axis=0))


def kernel(eta, p_hbm, c_hbm, o_ref, n_ref, g, cent, acc, ld, *rest):
    chunks = len(SIZES)
    s, ra, rb = rest[:chunks], rest[chunks:2 * chunks], rest[2 * chunks:3 * chunks]
    (
        load_sem, cent_sem, q_recv, f_recv, d_send, sh_send, sh_recv, sib_send, sib_recv,
        a_send, a_recv, b_send, b_recv,
    ) = rest[3 * chunks:]
    count, width = p_hbm.shape
    held = cent.shape[0]
    lanes = 128
    quarter = width // 4
    b = lax.axis_index("blk")
    l = lax.axis_index("loop")
    xh, y, c = b // 8, (b // 2) % 4, b % 2
    xl, z = l // 8, l % 8
    up, down, far = (y + 1) % 4, (y + 3) % 4, (y + 2) % 4
    ox, ol = 1 - xh, 1 - xl
    sc = 1 - c
    shard = xh * 4 + y

    def blk_of(hi, yy):
        return (hi * 4 + yy) * 2 + c

    def first_row(k):
        return NB * sum(SIZES[:k])

    def shard_rows(k, hi, yy):
        rows = SIZES[k]
        return pl.ds(pl.multiple_of(first_row(k) + c * (8 * rows) + (hi * 4 + yy) * rows, 16), rows)

    def core_rows(k, core):
        rows = SIZES[k]
        return pl.ds(pl.multiple_of(first_row(k) + core * (8 * rows), 16), 8 * rows)

    def cols_quarter(kind):
        return pl.ds(pl.multiple_of(kind * quarter, quarter), quarter)

    loop_order = [4, 12, 3, 5, 11, 13, 2, 6, 10, 14, 1, 7, 9, 15, 8]
    blk_order = [12, 4, 11, 13, 3, 5, 8, 9, 10, 14, 2, 6, 7, 15, 1]
    loop_peers = [(b, (l + j) % NB) for j in loop_order]
    blk_peers = [((b + j) % NB, l) for j in blk_order]
    x_loop = ol * 8 + z
    x_peers = [(blk_of(ox, (y + j) % 4), x_loop) for j in (2, 1, 3, 0)]
    barrier = pltpu.get_barrier_semaphore()
    for peer in x_peers + blk_peers[::-1] + loop_peers[::-1]:
        pl.semaphore_signal(barrier, inc=1, device_id=peer, device_id_type=MESH)
    for k, rows in enumerate(SIZES):
        pltpu.make_async_copy(
            p_hbm.at[pl.ds(sum(SIZES[:k]), rows)], g.at[shard_rows(k, xh, y)], load_sem
        ).start()
    cent_copy = pltpu.make_async_copy(c_hbm, cent, cent_sem)
    cent_copy.start()

    pl.semaphore_wait(barrier, 2 * (NB - 1) + 4)

    def wait_bytes(like, sem):
        pltpu.make_async_copy(like, like, sem).wait()

    def send(piece, send_sem, recv_sem, peer, source=None):
        pltpu.make_async_remote_copy(
            src_ref=piece if source is None else source, dst_ref=piece, send_sem=send_sem, recv_sem=recv_sem,
            device_id=peer, device_id_type=MESH,
        ).start()

    my_quarter = cols_quarter((z + 2 * xl) % 4)
    x_quarter = cols_quarter((z + 2 * ol) % 4)
    parted = [
        ((blk_of(ox, down), x_loop), x_quarter, (ox, up)),
        ((blk_of(ox, up), x_loop), x_quarter, (ox, down)),
        ((blk_of(ox, far), x_loop), x_quarter, (ox, far)),
        ((blk_of(xh, far), l), my_quarter, (xh, far)),
    ]
    near = [(blk_of(xh, down), l), (blk_of(xh, up), l), (blk_of(ox, y), x_loop)]
    sharers = [(b, xl * 8 + (z + 1) % 8), (b, xl * 8 + (z + 7) % 8), (b, x_loop)]
    sibling = (b + 1 - 2 * c, l)

    def own_rows(k):
        return p_hbm.at[pl.ds(sum(SIZES[:k]), SIZES[k])]

    def start_parted(k):
        for i, (peer, cols, _) in enumerate(parted):
            send(g.at[shard_rows(k, xh, y), cols], d_send.at[k], q_recv.at[k, i], peer, own_rows(k).at[:, cols])

    def start_near(k):
        for peer in near:
            send(g.at[shard_rows(k, xh, y)], d_send.at[k], f_recv.at[k], peer, own_rows(k))

    def share(k):
        for i, (_, _, source) in enumerate(parted):
            piece = g.at[shard_rows(k, *source), my_quarter]
            wait_bytes(piece, q_recv.at[k, i])
            for peer in sharers:
                send(piece, sh_send.at[k], sh_recv.at[k], peer)

    def to_sibling(k):
        wait_bytes(g.at[pl.ds(0, 3 * SIZES[k])], sh_recv.at[k])
        for place in ((ox, up), (ox, down), (ox, far), (xh, far)):
            send(g.at[shard_rows(k, *place)], sib_send.at[k], sib_recv.at[k], sibling)
        wait_bytes(g.at[pl.ds(0, 3 * SIZES[k])], f_recv.at[k])
        for place in ((xh, y), (xh, up), (xh, down), (ox, y)):
            send(g.at[shard_rows(k, *place)], sib_send.at[k], sib_recv.at[k], sibling)

    tile = 256

    def scores(k, core):
        part = 8 * SIZES[k]
        top, total = None, None
        for m0 in range(0, held, tile):
            t = lax.dot_general(
                cent[m0:m0 + tile, :], g[core_rows(k, core), :], NT, preferred_element_type=jnp.float32
            )
            t = t * SCALE
            s[k][core, m0:m0 + tile, :] = t
            t = t.reshape(tile // 8, 8, part)
            high = jnp.max(t, axis=0)
            new = high if top is None else jnp.maximum(top, high)
            add = jnp.sum(jnp.exp2(t - new[None]), axis=0)
            total = add if total is None else total * jnp.exp2(top - new) + add
            top = new
        peak = jnp.max(top, axis=0, keepdims=True)
        lse = peak + jnp.log2(jnp.sum(total * jnp.exp2(top - peak), axis=0, keepdims=True))
        for q in range(part // lanes):
            ra[k][l, core, q:q + 1, :] = lse[:, q * lanes:(q + 1) * lanes]

    def sibling_scores(k):
        wait_bytes(g.at[core_rows(k, sc)], sib_recv.at[k])
        scores(k, sc)

    def tell(k):
        for peer in loop_peers:
            send(ra[k].at[l], a_send.at[k], a_recv.at[k], peer)

    def first_merge(k):
        wait_bytes(ra[k].at[pl.ds(0, NB - 1)], a_recv.at[k])
        rb[k][b] = merge(ra[k][...])
        for peer in blk_peers:
            send(rb[k].at[b], b_send.at[k], b_recv.at[k], peer)

    def sums(k):
        rows = SIZES[k]
        part = 8 * rows
        groups = part // lanes
        wait_bytes(rb[k].at[pl.ds(0, NB - 1)], b_recv.at[k])
        norm = merge(rb[k][...])
        lines = [
            jnp.concatenate([norm[h, q:q + 1, :] for q in range(groups)], axis=1) for h in range(2)
        ]
        for m0 in range(0, held, tile):
            at = pl.ds(m0, tile)
            w = jnp.concatenate([jnp.exp2(s[k][h, at, :] - lines[h]) for h in range(2)], axis=1)
            load = w[:, 0:lanes]
            for q in range(1, 2 * groups):
                load = load + w[:, q * lanes:(q + 1) * lanes]
            add = jnp.dot(
                w.astype(jnp.bfloat16), g[pl.ds(first_row(k), NB * rows), :],
                preferred_element_type=jnp.float32,
            )
            if k > 0:
                load = load + ld[at, :]
                add = add + acc[at, :]
            if k < chunks - 1:
                ld[at, :] = load
                acc[at, :] = add
            else:
                scale = 1.0 / (1.0 + eta * jnp.sum(load, axis=1, keepdims=True))
                fresh = (cent[at, :].astype(jnp.float32) + eta * add) * scale
                o_ref[at, :] = fresh.astype(jnp.bfloat16)
        line = jnp.where(c == 0, lines[0], lines[1])
        for bit in range(3):
            turned = pltpu.roll(line, part - (rows << bit), 1)
            line = jnp.where((shard // (1 << bit)) % 2 == 1, turned, line)
        start = sum(SIZES[:k])
        n_ref[:, start:start + rows] = line[:, 0:rows] * LN2

    for kind, k in STARTS:
        start_parted(k) if kind == "Q" else start_near(k)
    wait_bytes(p_hbm, load_sem)
    cent_copy.wait()
    actions = dict(
        share=share, own=lambda k: scores(k, c), sib=sibling_scores, tell=tell,
        merge=first_merge, sums=sums,
    )
    actions["pass"] = to_sibling
    for kind, k in STEPS:
        actions[kind](k)

    for k, rows in enumerate(SIZES):
        wait_bytes(g.at[pl.ds(0, 4 * rows)], d_send.at[k])
        wait_bytes(g.at[pl.ds(0, 3 * rows)], sh_send.at[k])
        wait_bytes(g.at[core_rows(k, c)], sib_send.at[k])
        wait_bytes(ra[k].at[pl.ds(0, NB - 1)], a_send.at[k])
        wait_bytes(rb[k].at[pl.ds(0, NB - 1)], b_send.at[k])


def per_device(points, centroids):
    count, width = points.shape
    held = centroids.shape[0]
    total = count * NB
    eta = float(held * NB * NB) / float(total)
    chunks = len(SIZES)
    dma = pltpu.SemaphoreType.DMA
    hbm = pl.BlockSpec(memory_space=pltpu.HBM)
    vmem = pl.BlockSpec(memory_space=pltpu.VMEM)
    stats = [pltpu.VMEM((NB, 2, 8 * rows // 128, 128), jnp.float32) for rows in SIZES]
    each = dma((chunks,))
    fresh, norm = pl.pallas_call(
        functools.partial(kernel, eta),
        out_shape=(
            jax.ShapeDtypeStruct((held, width), jnp.bfloat16),
            jax.ShapeDtypeStruct((1, count), jnp.float32),
        ),
        in_specs=[hbm, hbm],
        out_specs=(vmem, vmem),
        scratch_shapes=[
            pltpu.VMEM((total, width), jnp.bfloat16),
            pltpu.VMEM((held, width), jnp.bfloat16),
            pltpu.VMEM((held, width), jnp.float32),
            pltpu.VMEM((held, 128), jnp.float32),
            *[pltpu.VMEM((2, held, 8 * rows), jnp.float32) for rows in SIZES],
            *stats, *stats,
            dma, dma,
            dma((chunks, 4)), each, each,
            each, each, each, each,
            each, each, each, each,
        ],
        compiler_params=pltpu.CompilerParams(
            collective_id=0, has_side_effects=True, vmem_limit_bytes=51 * 1024 * 1024
        ),
        cost_estimate=pl.CostEstimate(
            flops=4 * total * held * width, bytes_accessed=6 * held * width, transcendentals=2 * total * held
        ),
    )(points, centroids)
    return fresh, norm.reshape(count)


def solution(mesh):
    placed = (P("blk", None), P(("blk", "loop"), None))
    return jax.shard_map(
        per_device,
        mesh=mesh,
        in_specs=placed,
        out_specs=(P(("blk", "loop"), None), P("blk")),
        check_vma=False,
    )
```

```python
import functools

import jax
import jax.numpy as jnp
from jax import lax
from jax.experimental import pallas as pl
from jax.experimental.pallas import tpu as pltpu
from jax.sharding import PartitionSpec as P

MESH = pl.DeviceIdType.MESH
NT = (((1,), (1,)), ((), ()))
LOG2E = 1.4426950408889634
LN2 = 0.6931471805599453
SCALE = 20.0 * LOG2E
WRITES = 4
NB = 16
SIZES = (64, 64, 64)
STARTS = (("Q", 0), ("Q", 1), ("Q", 2), ("F", 0), ("F", 1), ("F", 2))
STEPS = (
    ("share", 0),
    ("share", 1),
    ("share", 2),
    ("pass", 0),
    ("own", 0),
    ("pass", 1),
    ("sib", 0),
    ("tell", 0),
    ("own", 1),
    ("pass", 2),
    ("sib", 1),
    ("tell", 1),
    ("own", 2),
    ("sib", 2),
    ("tell", 2),
    ("merge", 0),
    ("merge", 1),
    ("merge", 2),
    ("sums", 0),
    ("sums", 1),
    ("sums", 2),
)

def merge(parts):
    top = jnp.max(parts, axis=0)
    return top + jnp.log2(jnp.sum(jnp.exp2(parts - top[None]), axis=0))


def kernel(eta, p_hbm, c_hbm, o_ref, n_ref, g, cent, acc, ld, *rest):
    chunks = len(SIZES)
    s, ra, rb = rest[:chunks], rest[chunks:2 * chunks], rest[2 * chunks:3 * chunks]
    (
        load_sem, cent_sem, q_recv, f_recv, d_send, sh_send, sh_recv, sib_send, sib_recv,
        a_send, a_recv, b_send, b_recv,
    ) = rest[3 * chunks:]
    count, width = p_hbm.shape
    held = cent.shape[0]
    lanes = 128
    quarter = width // 4
    b = lax.axis_index("blk")
    l = lax.axis_index("loop")
    xh, y, c = b // 8, (b // 2) % 4, b % 2
    xl, z = l // 8, l % 8
    up, down, far = (y + 1) % 4, (y + 3) % 4, (y + 2) % 4
    ox, ol = 1 - xh, 1 - xl
    sc = 1 - c
    shard = xh * 4 + y

    def blk_of(hi, yy):
        return (hi * 4 + yy) * 2 + c

    def first_row(k):
        return NB * sum(SIZES[:k])

    def shard_rows(k, hi, yy):
        rows = SIZES[k]
        return pl.ds(pl.multiple_of(first_row(k) + c * (8 * rows) + (hi * 4 + yy) * rows, 16), rows)

    def core_rows(k, core):
        rows = SIZES[k]
        return pl.ds(pl.multiple_of(first_row(k) + core * (8 * rows), 16), 8 * rows)

    def cols_quarter(kind):
        return pl.ds(pl.multiple_of(kind * quarter, quarter), quarter)

    loop_order = [4, 12, 3, 5, 11, 13, 2, 6, 10, 14, 1, 7, 9, 15, 8]
    blk_order = [12, 4, 11, 13, 3, 5, 8, 9, 10, 14, 2, 6, 7, 15, 1]
    loop_peers = [(b, (l + j) % NB) for j in loop_order]
    blk_peers = [((b + j) % NB, l) for j in blk_order]
    x_loop = ol * 8 + z
    x_peers = [(blk_of(ox, (y + j) % 4), x_loop) for j in (2, 1, 3, 0)]
    barrier = pltpu.get_barrier_semaphore()
    for peer in x_peers + blk_peers[::-1] + loop_peers[::-1]:
        pl.semaphore_signal(barrier, inc=1, device_id=peer, device_id_type=MESH)
    for k, rows in enumerate(SIZES):
        pltpu.make_async_copy(
            p_hbm.at[pl.ds(sum(SIZES[:k]), rows)], g.at[shard_rows(k, xh, y)], load_sem
        ).start()
    cent_copy = pltpu.make_async_copy(c_hbm, cent, cent_sem)
    cent_copy.start()

    pl.semaphore_wait(barrier, 2 * (NB - 1) + 4)

    def wait_bytes(like, sem):
        pltpu.make_async_copy(like, like, sem).wait()

    def send(piece, send_sem, recv_sem, peer, source=None):
        pltpu.make_async_remote_copy(
            src_ref=piece if source is None else source, dst_ref=piece, send_sem=send_sem, recv_sem=recv_sem,
            device_id=peer, device_id_type=MESH,
        ).start()

    my_quarter = cols_quarter((z + 2 * xl) % 4)
    x_quarter = cols_quarter((z + 2 * ol) % 4)
    parted = [
        ((blk_of(ox, down), x_loop), x_quarter, (ox, up)),
        ((blk_of(ox, up), x_loop), x_quarter, (ox, down)),
        ((blk_of(ox, far), x_loop), x_quarter, (ox, far)),
        ((blk_of(xh, far), l), my_quarter, (xh, far)),
    ]
    near = [(blk_of(xh, down), l), (blk_of(xh, up), l), (blk_of(ox, y), x_loop)]
    sharers = [(b, xl * 8 + (z + 1) % 8), (b, xl * 8 + (z + 7) % 8), (b, x_loop)]
    sibling = (b + 1 - 2 * c, l)

    def own_rows(k):
        return p_hbm.at[pl.ds(sum(SIZES[:k]), SIZES[k])]

    def start_parted(k):
        for i, (peer, cols, _) in enumerate(parted):
            send(g.at[shard_rows(k, xh, y), cols], d_send.at[k], q_recv.at[k, i], peer, own_rows(k).at[:, cols])

    def start_near(k):
        for peer in near:
            send(g.at[shard_rows(k, xh, y)], d_send.at[k], f_recv.at[k], peer, own_rows(k))

    def share(k):
        for i, (_, _, source) in enumerate(parted):
            piece = g.at[shard_rows(k, *source), my_quarter]
            wait_bytes(piece, q_recv.at[k, i])
            for peer in sharers:
                send(piece, sh_send.at[k], sh_recv.at[k], peer)

    def to_sibling(k):
        wait_bytes(g.at[pl.ds(0, 3 * SIZES[k])], sh_recv.at[k])
        for place in ((ox, up), (ox, down), (ox, far), (xh, far)):
            send(g.at[shard_rows(k, *place)], sib_send.at[k], sib_recv.at[k], sibling)
        wait_bytes(g.at[pl.ds(0, 3 * SIZES[k])], f_recv.at[k])
        for place in ((xh, y), (xh, up), (xh, down), (ox, y)):
            send(g.at[shard_rows(k, *place)], sib_send.at[k], sib_recv.at[k], sibling)

    tile = 256

    def scores(k, core):
        part = 8 * SIZES[k]
        top, total = None, None
        for m0 in range(0, held, tile):
            t = lax.dot_general(
                cent[m0:m0 + tile, :], g[core_rows(k, core), :], NT, preferred_element_type=jnp.float32
            )
            t = t * SCALE
            s[k][core, m0:m0 + tile, :] = t
            t = t.reshape(tile // 8, 8, part)
            high = jnp.max(t, axis=0)
            new = high if top is None else jnp.maximum(top, high)
            add = jnp.sum(jnp.exp2(t - new[None]), axis=0)
            total = add if total is None else total * jnp.exp2(top - new) + add
            top = new
        peak = jnp.max(top, axis=0, keepdims=True)
        lse = peak + jnp.log2(jnp.sum(total * jnp.exp2(top - peak), axis=0, keepdims=True))
        for q in range(part // lanes):
            ra[k][l, core, q:q + 1, :] = lse[:, q * lanes:(q + 1) * lanes]

    def sibling_scores(k):
        wait_bytes(g.at[core_rows(k, sc)], sib_recv.at[k])
        scores(k, sc)

    def tell(k):
        for peer in loop_peers:
            send(ra[k].at[l], a_send.at[k], a_recv.at[k], peer)

    def first_merge(k):
        wait_bytes(ra[k].at[pl.ds(0, NB - 1)], a_recv.at[k])
        rb[k][b] = merge(ra[k][...])
        for peer in blk_peers:
            send(rb[k].at[b], b_send.at[k], b_recv.at[k], peer)

    def sums(k):
        rows = SIZES[k]
        part = 8 * rows
        groups = part // lanes
        wait_bytes(rb[k].at[pl.ds(0, NB - 1)], b_recv.at[k])
        norm = merge(rb[k][...])
        lines = [
            jnp.concatenate([norm[h, q:q + 1, :] for q in range(groups)], axis=1) for h in range(2)
        ]
        for m0 in range(0, held, tile):
            at = pl.ds(m0, tile)
            w = jnp.concatenate([jnp.exp2(s[k][h, at, :] - lines[h]) for h in range(2)], axis=1)
            load = w[:, 0:lanes]
            for q in range(1, 2 * groups):
                load = load + w[:, q * lanes:(q + 1) * lanes]
            add = jnp.dot(
                w.astype(jnp.bfloat16), g[pl.ds(first_row(k), NB * rows), :],
                preferred_element_type=jnp.float32,
            )
            if k > 0:
                load = load + ld[at, :]
                add = add + acc[at, :]
            if k < chunks - 1:
                ld[at, :] = load
                acc[at, :] = add
            else:
                scale = 1.0 / (1.0 + eta * jnp.sum(load, axis=1, keepdims=True))
                fresh = (cent[at, :].astype(jnp.float32) + eta * add) * scale
                o_ref[at, :] = fresh.astype(jnp.bfloat16)
        line = jnp.where(c == 0, lines[0], lines[1])
        for bit in range(3):
            turned = pltpu.roll(line, part - (rows << bit), 1)
            line = jnp.where((shard // (1 << bit)) % 2 == 1, turned, line)
        start = sum(SIZES[:k])
        n_ref[:, start:start + rows] = line[:, 0:rows] * LN2

    for kind, k in STARTS:
        start_parted(k) if kind == "Q" else start_near(k)
    wait_bytes(p_hbm, load_sem)
    cent_copy.wait()
    actions = dict(
        share=share, own=lambda k: scores(k, c), sib=sibling_scores, tell=tell,
        merge=first_merge, sums=sums,
    )
    actions["pass"] = to_sibling
    for kind, k in STEPS:
        actions[kind](k)

    for k, rows in enumerate(SIZES):
        wait_bytes(g.at[pl.ds(0, 4 * rows)], d_send.at[k])
        wait_bytes(g.at[pl.ds(0, 3 * rows)], sh_send.at[k])
        wait_bytes(g.at[core_rows(k, c)], sib_send.at[k])
        wait_bytes(ra[k].at[pl.ds(0, NB - 1)], a_send.at[k])
        wait_bytes(rb[k].at[pl.ds(0, NB - 1)], b_send.at[k])


def write_out(fresh, norm, fresh_out, norm_out, sems):
    rows = fresh.shape[0] // WRITES
    copies = [pltpu.make_async_copy(norm, norm_out, sems.at[WRITES])]
    for i in range(WRITES):
        at = pl.ds(i * rows, rows)
        copies.append(pltpu.make_async_copy(fresh.at[at], fresh_out.at[at], sems.at[i]))
    for copy in copies:
        copy.start()
    for copy in copies:
        copy.wait()


def per_device(points, centroids):
    count, width = points.shape
    held = centroids.shape[0]
    total = count * NB
    eta = float(held * NB * NB) / float(total)
    chunks = len(SIZES)
    dma = pltpu.SemaphoreType.DMA
    hbm = pl.BlockSpec(memory_space=pltpu.HBM)
    vmem = pl.BlockSpec(memory_space=pltpu.VMEM)
    anywhere = pl.BlockSpec(memory_space=pl.ANY)
    stats = [pltpu.VMEM((NB, 2, 8 * rows // 128, 128), jnp.float32) for rows in SIZES]
    each = dma((chunks,))
    fresh, norm = pl.pallas_call(
        functools.partial(kernel, eta),
        out_shape=(
            jax.ShapeDtypeStruct((held, width), jnp.bfloat16),
            jax.ShapeDtypeStruct((1, count), jnp.float32),
        ),
        in_specs=[hbm, hbm],
        out_specs=(vmem, vmem),
        scratch_shapes=[
            pltpu.VMEM((total, width), jnp.bfloat16),
            pltpu.VMEM((held, width), jnp.bfloat16),
            pltpu.VMEM((held, width), jnp.float32),
            pltpu.VMEM((held, 128), jnp.float32),
            *[pltpu.VMEM((2, held, 8 * rows), jnp.float32) for rows in SIZES],
            *stats, *stats,
            dma, dma,
            dma((chunks, 4)), each, each,
            each, each, each, each,
            each, each, each, each,
        ],
        compiler_params=pltpu.CompilerParams(
            collective_id=0, has_side_effects=True, vmem_limit_bytes=51 * 1024 * 1024
        ),
        cost_estimate=pl.CostEstimate(
            flops=4 * total * held * width, bytes_accessed=6 * held * width, transcendentals=2 * total * held
        ),
    )(points, centroids)
    fresh, norm = pl.pallas_call(
        write_out,
        out_shape=(
            jax.ShapeDtypeStruct((held, width), jnp.bfloat16),
            jax.ShapeDtypeStruct((1, count), jnp.float32),
        ),
        in_specs=[vmem, vmem],
        out_specs=(anywhere, anywhere),
        scratch_shapes=[dma((WRITES + 1,))],
        compiler_params=pltpu.CompilerParams(vmem_limit_bytes=8 * 1024 * 1024),
    )(fresh, norm)
    return fresh, norm.reshape(count)


def solution(mesh):
    placed = (P("blk", None), P(("blk", "loop"), None))
    return jax.shard_map(
        per_device,
        mesh=mesh,
        in_specs=placed,
        out_specs=(P(("blk", "loop"), None), P("blk")),
        check_vma=False,
    )
```

```python
import functools

import jax
import jax.numpy as jnp
from jax import lax
from jax.experimental import pallas as pl
from jax.experimental.pallas import tpu as pltpu
from jax.sharding import PartitionSpec as P

MESH = pl.DeviceIdType.MESH
NT = (((1,), (1,)), ((), ()))
LOG2E = 1.4426950408889634
LN2 = 0.6931471805599453
SCALE = 20.0 * LOG2E
WRITES = 4
GREETINGS = 4
NB = 16
SIZES = (64, 64, 64)
STARTS = (("Q", 0), ("Q", 1), ("Q", 2), ("F", 0), ("F", 1), ("F", 2))
STEPS = (
    ("greet", 0),
    ("share", 0),
    ("greet", 1),
    ("share", 1),
    ("greet", 2),
    ("share", 2),
    ("greet", 3),
    ("pass", 0),
    ("greet", 4),
    ("own", 0),
    ("pass", 1),
    ("sib", 0),
    ("tell", 0),
    ("own", 1),
    ("pass", 2),
    ("sib", 1),
    ("tell", 1),
    ("own", 2),
    ("sib", 2),
    ("tell", 2),
    ("merge", 0),
    ("merge", 1),
    ("merge", 2),
    ("sums", 0),
    ("sums", 1),
    ("sums", 2),
)

def merge(parts):
    top = jnp.max(parts, axis=0)
    return top + jnp.log2(jnp.sum(jnp.exp2(parts - top[None]), axis=0))


def kernel(eta, p_hbm, c_hbm, o_ref, n_ref, g, cent, acc, ld, *rest):
    chunks = len(SIZES)
    s, ra, rb = rest[:chunks], rest[chunks:2 * chunks], rest[2 * chunks:3 * chunks]
    (
        met, load_sem, cent_sem, q_recv, f_recv, d_send, sh_send, sh_recv, sib_send, sib_recv,
        a_send, a_recv, b_send, b_recv,
    ) = rest[3 * chunks:]
    count, width = p_hbm.shape
    held = cent.shape[0]
    lanes = 128
    quarter = width // 4
    b = lax.axis_index("blk")
    l = lax.axis_index("loop")
    xh, y, c = b // 8, (b // 2) % 4, b % 2
    xl, z = l // 8, l % 8
    up, down, far = (y + 1) % 4, (y + 3) % 4, (y + 2) % 4
    ox, ol = 1 - xh, 1 - xl
    sc = 1 - c
    shard = xh * 4 + y

    def blk_of(hi, yy):
        return (hi * 4 + yy) * 2 + c

    def first_row(k):
        return NB * sum(SIZES[:k])

    def shard_rows(k, hi, yy):
        rows = SIZES[k]
        return pl.ds(pl.multiple_of(first_row(k) + c * (8 * rows) + (hi * 4 + yy) * rows, 16), rows)

    def core_rows(k, core):
        rows = SIZES[k]
        return pl.ds(pl.multiple_of(first_row(k) + core * (8 * rows), 16), 8 * rows)

    def cols_quarter(kind):
        return pl.ds(pl.multiple_of(kind * quarter, quarter), quarter)

    loop_order = [4, 12, 3, 5, 11, 13, 2, 6, 10, 14, 1, 7, 9, 15, 8]
    blk_order = [12, 4, 11, 13, 3, 5, 8, 9, 10, 14, 2, 6, 7, 15, 1]
    loop_peers = [(b, (l + j) % NB) for j in loop_order]
    blk_peers = [((b + j) % NB, l) for j in blk_order]
    x_loop = ol * 8 + z
    x_peers = [(blk_of(ox, (y + j) % 4), x_loop) for j in (2, 1, 3, 0)]
    barrier = pltpu.get_barrier_semaphore()
    z_up, z_down = (b, xl * 8 + (z + 1) % 8), (b, xl * 8 + (z + 7) % 8)
    sibling = (b + 1 - 2 * c, l)
    close = [z_up, z_down, (b, x_loop), sibling]
    first = close + x_peers + [(blk_of(xh, far), l), (blk_of(xh, up), l), (blk_of(xh, down), l)]
    for peer in first:
        pl.semaphore_signal(barrier, inc=1, device_id=peer, device_id_type=MESH)

    for k, rows in enumerate(SIZES):
        pltpu.make_async_copy(
            p_hbm.at[pl.ds(sum(SIZES[:k]), rows)], g.at[shard_rows(k, xh, y)], load_sem
        ).start()
    cent_copy = pltpu.make_async_copy(c_hbm, cent, cent_sem)
    cent_copy.start()

    pl.semaphore_wait(barrier, len(first))

    def greet(turn):
        if turn > 0:
            pl.semaphore_wait(met.at[turn - 1], len(close))
        if turn < GREETINGS:
            for peer in close:
                pl.semaphore_signal(met.at[turn], inc=1, device_id=peer, device_id_type=MESH)

    def wait_bytes(like, sem):
        pltpu.make_async_copy(like, like, sem).wait()

    def send(piece, send_sem, recv_sem, peer, source=None):
        pltpu.make_async_remote_copy(
            src_ref=piece if source is None else source, dst_ref=piece, send_sem=send_sem, recv_sem=recv_sem,
            device_id=peer, device_id_type=MESH,
        ).start()

    my_quarter = cols_quarter((z + 2 * xl) % 4)
    x_quarter = cols_quarter((z + 2 * ol) % 4)
    parted = [
        ((blk_of(ox, down), x_loop), x_quarter, (ox, up)),
        ((blk_of(ox, up), x_loop), x_quarter, (ox, down)),
        ((blk_of(ox, far), x_loop), x_quarter, (ox, far)),
        ((blk_of(xh, far), l), my_quarter, (xh, far)),
    ]
    near = [(blk_of(xh, down), l), (blk_of(xh, up), l), (blk_of(ox, y), x_loop)]
    sharers = [z_up, z_down, (b, x_loop)]

    def own_rows(k):
        return p_hbm.at[pl.ds(sum(SIZES[:k]), SIZES[k])]

    def start_parted(k):
        for i, (peer, cols, _) in enumerate(parted):
            send(g.at[shard_rows(k, xh, y), cols], d_send.at[k], q_recv.at[k, i], peer, own_rows(k).at[:, cols])

    def start_near(k):
        for peer in near:
            send(g.at[shard_rows(k, xh, y)], d_send.at[k], f_recv.at[k], peer, own_rows(k))

    def share(k):
        for i, (_, _, source) in enumerate(parted):
            piece = g.at[shard_rows(k, *source), my_quarter]
            wait_bytes(piece, q_recv.at[k, i])
            for peer in sharers:
                send(piece, sh_send.at[k], sh_recv.at[k], peer)

    def to_sibling(k):
        wait_bytes(g.at[pl.ds(0, 3 * SIZES[k])], sh_recv.at[k])
        for place in ((ox, up), (ox, down), (ox, far), (xh, far)):
            send(g.at[shard_rows(k, *place)], sib_send.at[k], sib_recv.at[k], sibling)
        wait_bytes(g.at[pl.ds(0, 3 * SIZES[k])], f_recv.at[k])
        for place in ((xh, y), (xh, up), (xh, down), (ox, y)):
            send(g.at[shard_rows(k, *place)], sib_send.at[k], sib_recv.at[k], sibling)

    tile = 256

    def scores(k, core):
        part = 8 * SIZES[k]
        top, total = None, None
        for m0 in range(0, held, tile):
            t = lax.dot_general(
                cent[m0:m0 + tile, :], g[core_rows(k, core), :], NT, preferred_element_type=jnp.float32
            )
            t = t * SCALE
            s[k][core, m0:m0 + tile, :] = t
            t = t.reshape(tile // 8, 8, part)
            high = jnp.max(t, axis=0)
            new = high if top is None else jnp.maximum(top, high)
            add = jnp.sum(jnp.exp2(t - new[None]), axis=0)
            total = add if total is None else total * jnp.exp2(top - new) + add
            top = new
        peak = jnp.max(top, axis=0, keepdims=True)
        lse = peak + jnp.log2(jnp.sum(total * jnp.exp2(top - peak), axis=0, keepdims=True))
        for q in range(part // lanes):
            ra[k][l, core, q:q + 1, :] = lse[:, q * lanes:(q + 1) * lanes]

    def sibling_scores(k):
        wait_bytes(g.at[core_rows(k, sc)], sib_recv.at[k])
        scores(k, sc)

    def tell(k):
        for peer in loop_peers:
            send(ra[k].at[l], a_send.at[k], a_recv.at[k], peer)

    def first_merge(k):
        wait_bytes(ra[k].at[pl.ds(0, NB - 1)], a_recv.at[k])
        rb[k][b] = merge(ra[k][...])
        for peer in blk_peers:
            send(rb[k].at[b], b_send.at[k], b_recv.at[k], peer)

    def sums(k):
        rows = SIZES[k]
        part = 8 * rows
        groups = part // lanes
        wait_bytes(rb[k].at[pl.ds(0, NB - 1)], b_recv.at[k])
        norm = merge(rb[k][...])
        lines = [
            jnp.concatenate([norm[h, q:q + 1, :] for q in range(groups)], axis=1) for h in range(2)
        ]
        for m0 in range(0, held, tile):
            at = pl.ds(m0, tile)
            w = jnp.concatenate([jnp.exp2(s[k][h, at, :] - lines[h]) for h in range(2)], axis=1)
            load = w[:, 0:lanes]
            for q in range(1, 2 * groups):
                load = load + w[:, q * lanes:(q + 1) * lanes]
            add = jnp.dot(
                w.astype(jnp.bfloat16), g[pl.ds(first_row(k), NB * rows), :],
                preferred_element_type=jnp.float32,
            )
            if k > 0:
                load = load + ld[at, :]
                add = add + acc[at, :]
            if k < chunks - 1:
                ld[at, :] = load
                acc[at, :] = add
            else:
                scale = 1.0 / (1.0 + eta * jnp.sum(load, axis=1, keepdims=True))
                fresh = (cent[at, :].astype(jnp.float32) + eta * add) * scale
                o_ref[at, :] = fresh.astype(jnp.bfloat16)
        line = jnp.where(c == 0, lines[0], lines[1])
        for bit in range(3):
            turned = pltpu.roll(line, part - (rows << bit), 1)
            line = jnp.where((shard // (1 << bit)) % 2 == 1, turned, line)
        start = sum(SIZES[:k])
        n_ref[:, start:start + rows] = line[:, 0:rows] * LN2

    for kind, k in STARTS:
        start_parted(k) if kind == "Q" else start_near(k)
    wait_bytes(p_hbm, load_sem)
    cent_copy.wait()
    actions = dict(
        share=share, own=lambda k: scores(k, c), sib=sibling_scores, tell=tell,
        merge=first_merge, sums=sums, greet=greet,
    )
    actions["pass"] = to_sibling
    for kind, k in STEPS:
        actions[kind](k)

    for k, rows in enumerate(SIZES):
        wait_bytes(g.at[pl.ds(0, 4 * rows)], d_send.at[k])
        wait_bytes(g.at[pl.ds(0, 3 * rows)], sh_send.at[k])
        wait_bytes(g.at[core_rows(k, c)], sib_send.at[k])
        wait_bytes(ra[k].at[pl.ds(0, NB - 1)], a_send.at[k])
        wait_bytes(rb[k].at[pl.ds(0, NB - 1)], b_send.at[k])


def write_out(fresh, norm, fresh_out, norm_out, sems):
    rows = fresh.shape[0] // WRITES
    copies = [pltpu.make_async_copy(norm, norm_out, sems.at[WRITES])]
    for i in range(WRITES):
        at = pl.ds(i * rows, rows)
        copies.append(pltpu.make_async_copy(fresh.at[at], fresh_out.at[at], sems.at[i]))
    for copy in copies:
        copy.start()
    for copy in copies:
        copy.wait()


def per_device(points, centroids):
    count, width = points.shape
    held = centroids.shape[0]
    total = count * NB
    eta = float(held * NB * NB) / float(total)
    chunks = len(SIZES)
    dma = pltpu.SemaphoreType.DMA
    hbm = pl.BlockSpec(memory_space=pltpu.HBM)
    vmem = pl.BlockSpec(memory_space=pltpu.VMEM)
    anywhere = pl.BlockSpec(memory_space=pl.ANY)
    stats = [pltpu.VMEM((NB, 2, 8 * rows // 128, 128), jnp.float32) for rows in SIZES]
    each = dma((chunks,))
    fresh, norm = pl.pallas_call(
        functools.partial(kernel, eta),
        out_shape=(
            jax.ShapeDtypeStruct((held, width), jnp.bfloat16),
            jax.ShapeDtypeStruct((1, count), jnp.float32),
        ),
        in_specs=[hbm, hbm],
        out_specs=(vmem, vmem),
        scratch_shapes=[
            pltpu.VMEM((total, width), jnp.bfloat16),
            pltpu.VMEM((held, width), jnp.bfloat16),
            pltpu.VMEM((held, width), jnp.float32),
            pltpu.VMEM((held, 128), jnp.float32),
            *[pltpu.VMEM((2, held, 8 * rows), jnp.float32) for rows in SIZES],
            *stats, *stats,
            pltpu.SemaphoreType.REGULAR((GREETINGS,)),
            dma, dma,
            dma((chunks, 4)), each, each,
            each, each, each, each,
            each, each, each, each,
        ],
        compiler_params=pltpu.CompilerParams(
            collective_id=0, has_side_effects=True, vmem_limit_bytes=51 * 1024 * 1024
        ),
        cost_estimate=pl.CostEstimate(
            flops=4 * total * held * width, bytes_accessed=6 * held * width, transcendentals=2 * total * held
        ),
    )(points, centroids)
    fresh, norm = pl.pallas_call(
        write_out,
        out_shape=(
            jax.ShapeDtypeStruct((held, width), jnp.bfloat16),
            jax.ShapeDtypeStruct((1, count), jnp.float32),
        ),
        in_specs=[vmem, vmem],
        out_specs=(anywhere, anywhere),
        scratch_shapes=[dma((WRITES + 1,))],
        compiler_params=pltpu.CompilerParams(vmem_limit_bytes=8 * 1024 * 1024),
    )(fresh, norm)
    return fresh, norm.reshape(count)


def solution(mesh):
    placed = (P("blk", None), P(("blk", "loop"), None))
    return jax.shard_map(
        per_device,
        mesh=mesh,
        in_specs=placed,
        out_specs=(P(("blk", "loop"), None), P("blk")),
        check_vma=False,
    )
```
